32 devices in a mesh: dp: 8 (over z, y), ty: 2 (over core), tz: 2 (over x).
Axes of the slice: x: 2, y: 2, z: 4, core: 2. Of those that a mesh axis runs over, the one named last changes fastest.
Arguments:
- inputs: bfloat16 [8, 4, 48, 48, 256], P('dp', None, 'ty', 'tz'), may hold values from -6 to 6
- pre_first: bfloat16 [8, 4, 48, 48, 256], P('dp', None, 'ty', 'tz'), may hold values from -6 to 6
- pre_second: bfloat16 [8, 4, 48, 48, 256], P('dp', None, 'ty', 'tz'), may hold values from -6 to 6
- grad_out: bfloat16 [8, 4, 48, 48, 256], P('dp', None, 'ty', 'tz'), may hold values from -6 to 6
- w_first: bfloat16 [256, 27, 256], P('dp'), may hold values from -0.078125 to 0.078125
- w_second: bfloat16 [256, 27, 256], P('dp'), may hold values from -0.078125 to 0.078125
Outputs:
- grad_input: bfloat16 [8, 4, 48, 48, 256], P('dp', None, 'ty', 'tz')
- grad_w_first: float32 [256, 27, 256], P('dp')
- grad_w_second: float32 [256, 27, 256], P('dp')
The draws below stay inside these ranges and needn't reach their ends.
All inputs are finite; a program needn't handle non-finite values.
Results may differ from the reference program's by a relative error of at most 0.0049.
Values may be sent and summed in bfloat16 or wider, within the bound.
A program may use at most 128 MiB of HBM per device.

```python
import math
import jax
import jax.numpy as jnp
from jax import lax

C = 256
TAPS = 27
DX = 4
NY = 48
NZ = 48
FRAMES = 8


def strengthened(result, own_key, source, target, blocks, factor):
    def block_of(position):
        return (jnp.arange(result.shape[position]) // (result.shape[position] // blocks)).reshape((-1,) + (1,) * (result.ndim - 1 - position))

    near = jax.random.permutation(own_key, blocks)[block_of(target)]
    other_side = (block_of(target) + blocks // 2) % blocks
    return jnp.where((block_of(source) == near) | (block_of(source) == other_side), factor * result, result)


def levels(own_key, extent, pieces, smallest, high):
    gain = 1.0
    for axis_at, parts in pieces:
        steps = jax.random.uniform(jax.random.fold_in(jax.random.fold_in(own_key, 6), axis_at), (parts,), jnp.float32, smallest / len(pieces), high / len(pieces))
        gain = gain * jnp.repeat(jnp.exp(steps), extent[axis_at] // parts).reshape((-1,) + (1,) * (len(extent) - 1 - axis_at))
    return gain


def noise(stream_key, dims, scale, limit, shards=(), kind=jnp.bfloat16):
    array = scale * jax.random.normal(stream_key, dims, jnp.float32)
    if shards:
        array = array * levels(stream_key, dims, shards, -0.22, 0.18)
    return jnp.clip(array, -limit, limit).astype(kind)


def gaussian_with(key, dims, scale, most, pieces, heavy, kind=jnp.bfloat16):
    values = scale * jax.random.normal(key, dims, jnp.float32)
    if pieces:
        values = values * levels(key, dims, pieces, -0.22, 0.18)
    return jnp.clip(strengthened(values, jax.random.fold_in(key, 3), *heavy), -most, most).astype(kind)


def setup_inputs(seed: int = 0) -> dict:
    streams_of = jax.random.split(jax.random.key(seed), 7)
    inputs = gaussian_with(streams_of[0], (FRAMES, DX, NY, NZ, C), 1.0, 6.0, ((0, 8), (2, 2), (3, 2)), (0, 4, 8, 2.0))
    pre_first = gaussian_with(streams_of[1], (FRAMES, DX, NY, NZ, C), 1.0, 6.0, ((0, 8), (2, 2), (3, 2)), (0, 4, 8, 2.0))
    pre_second = noise(streams_of[2], (FRAMES, DX, NY, NZ, C), 1.0, 6.0, ((0, 8), (2, 2), (3, 2)))
    grad_out = noise(streams_of[3], (FRAMES, DX, NY, NZ, C), 1.0, 6.0, ((0, 8), (2, 2), (3, 2)))
    w_first = noise(streams_of[4], (C, TAPS, C), (TAPS * C) ** -0.5, 0.078125, ((0, 8),))
    w_second = noise(streams_of[5], (C, TAPS, C), (TAPS * C) ** -0.5, 0.078125, ((0, 8),))
    return {"inputs": inputs, "pre_first": pre_first, "pre_second": pre_second, "grad_out": grad_out, "w_first": w_first, "w_second": w_second}


def make_offsets():
    return [(shift_a, shift_b, shift_c) for shift_a in (-1, 0, 1) for shift_b in (-1, 0, 1) for shift_c in (-1, 0, 1)]

def pad_space(field):
    return jnp.pad(field, ((0, 0), (1, 1), (1, 1), (1, 1), (0, 0)))

def window(padded, offset, shape):
    return padded[:, 1 + offset[0]:1 + offset[0] + shape[1], 1 + offset[1]:1 + offset[1] + shape[2], 1 + offset[2]:1 + offset[2] + shape[3], :]

def data_grad(grad, weight):
    shape = grad.shape
    width = shape[4]
    padded = pad_space(grad)
    total = jnp.zeros((shape[0] * shape[1] * shape[2] * shape[3], weight.shape[0]), jnp.float32)
    for index, offset in enumerate(make_offsets()):
        back = (-offset[0], -offset[1], -offset[2])
        piece = window(padded, back, shape).reshape(-1, width)
        total = total + lax.dot_general(piece, weight[:, index, :], (((1,), (1,)), ((), ())), preferred_element_type=jnp.float32)
    return total.reshape(shape[0], shape[1], shape[2], shape[3], -1)

def weight_grad(act, grad):
    shape = act.shape
    padded = pad_space(act)
    flat_grad = grad.reshape(-1, grad.shape[4])
    terms = []
    for index, offset in enumerate(make_offsets()):
        piece = window(padded, offset, shape).reshape(-1, shape[4])
        terms.append(lax.dot_general(piece, flat_grad, (((0,), (0,)), ((), ())), preferred_element_type=jnp.float32))
    return jnp.stack(terms, axis=1)

def reference(inputs, pre_first, pre_second, grad_out, w_first, w_second):
    shape = inputs.shape
    scale = 1.0 / math.sqrt(shape[0] * shape[1] * shape[2] * shape[3])
    grad_top = jnp.where(pre_second > 0, grad_out, jnp.zeros((), jnp.bfloat16))
    active = jnp.where(pre_first > 0, pre_first, jnp.zeros((), jnp.bfloat16))
    upstream = data_grad(grad_top, w_second)
    grad_low = jnp.where(pre_first > 0, upstream, jnp.zeros((), jnp.float32)).astype(jnp.bfloat16)
    grad_w_second = weight_grad(active, grad_top) * scale
    grad_w_first = weight_grad(inputs, grad_low) * scale
    grad_input = data_grad(grad_low, w_first).astype(jnp.bfloat16)
    return (grad_input, grad_w_first, grad_w_second)
```

```python
import math

import jax
import jax.numpy as jnp
from jax import lax
from jax.sharding import PartitionSpec as P


def extended(block, sides, width):
    for axis, dim in sides:
        count = lax.axis_size(axis)
        forward = [(i, i + 1) for i in range(count - 1)]
        backward = [(target, source) for source, target in forward]
        low = lax.ppermute(
            lax.slice_in_dim(block, block.shape[dim] - width, None, axis=dim), axis, forward
        )
        high = lax.ppermute(lax.slice_in_dim(block, 0, width, axis=dim), axis, backward)
        block = jnp.concatenate([low, block, high], axis=dim)
    return block


def data_grad(grad_pad, weight):
    ch_in, _, ch_out = weight.shape
    kernel = weight.reshape(ch_in, 3, 3, 3, ch_out)[:, ::-1, ::-1, ::-1, :]
    return lax.conv_general_dilated(
        grad_pad,
        kernel,
        (1, 1, 1),
        ((1, 1), (0, 0), (0, 0)),
        dimension_numbers=("NDHWC", "ODHWI", "NDHWC"),
        preferred_element_type=jnp.float32,
    )


def filter_grad(act_pad, grad):
    return lax.conv_general_dilated(
        act_pad,
        grad,
        (1, 1, 1),
        ((1, 1), (0, 0), (0, 0)),
        dimension_numbers=("CDHWN", "IDHWO", "NDHWC"),
        preferred_element_type=jnp.float32,
    ).reshape(act_pad.shape[4], -1, grad.shape[4])


def reduce_terms(partial_value):
    ch_in, tap_count, ch_out = partial_value.shape
    dp = lax.axis_size("dp")
    tile = lax.axis_size("ty") * lax.axis_size("tz")
    part = partial_value.astype(jnp.bfloat16).reshape(dp, tile, -1, ch_out)
    part = lax.psum_scatter(part, ("ty", "tz"), scatter_dimension=1, tiled=True)
    share = lax.psum_scatter(part, "dp", scatter_dimension=0, tiled=True)
    share = share.reshape(-1, ch_out)
    whole = lax.all_gather(share, ("ty", "tz"), axis=0, tiled=True)
    return whole.astype(jnp.float32).reshape(-1, tap_count, ch_out)


def local(inputs, pre_first, pre_second, grad_out, w_first, w_second):
    shape = grad_out.shape
    count = (
        shape[0]
        * shape[1]
        * shape[2]
        * shape[3]
        * lax.axis_size("dp")
        * lax.axis_size("ty")
        * lax.axis_size("tz")
    )
    scale = 1.0 / math.sqrt(count)
    sides = (("ty", 2), ("tz", 3))
    zero_half = jnp.zeros((), jnp.bfloat16)
    grad_top = jnp.where(pre_second > 0, grad_out, zero_half)
    active = jnp.where(pre_first > 0, pre_first, zero_half)
    whole_second = lax.all_gather(w_second, "dp", axis=0, tiled=True)
    whole_first = lax.all_gather(w_first, "dp", axis=0, tiled=True)
    part_second = filter_grad(extended(active, sides, 1), grad_top)
    grad_w_second = reduce_terms(part_second * scale)
    upstream = data_grad(extended(grad_top, sides, 1), whole_second)
    grad_low = jnp.where(pre_first > 0, upstream, jnp.zeros((), jnp.float32)).astype(jnp.bfloat16)
    part_first = filter_grad(extended(inputs, sides, 1), grad_low)
    grad_w_first = reduce_terms(part_first * scale)
    grad_input = data_grad(extended(grad_low, sides, 1), whole_first).astype(jnp.bfloat16)
    return (grad_input, grad_w_first, grad_w_second)


def solution(mesh):
    placed = (
        P("dp", None, "ty", "tz", None),
        P("dp", None, "ty", "tz", None),
        P("dp", None, "ty", "tz", None),
        P("dp", None, "ty", "tz", None),
        P("dp", None, None),
        P("dp", None, None),
    )
    return jax.shard_map(
        local,
        mesh=mesh,
        in_specs=placed,
        out_specs=(P("dp", None, "ty", "tz", None), P("dp", None, None), P("dp", None, None)),
        check_vma=False,
    )
```

```python
import functools
import math

import jax
import jax.numpy as jnp
from jax import lax
from jax.experimental import pallas as pl
from jax.experimental.pallas import tpu as pltpu
from jax.sharding import PartitionSpec as P

MESH = pl.DeviceIdType.MESH
VMEM = pl.BlockSpec(memory_space=pltpu.VMEM)
NT = (((1,), (1,)), ((), ()))


def extended(block, sides, width):
    for axis, dim in sides:
        count = lax.axis_size(axis)
        forward = [(i, i + 1) for i in range(count - 1)]
        backward = [(target, source) for source, target in forward]
        low = lax.ppermute(
            lax.slice_in_dim(block, block.shape[dim] - width, None, axis=dim), axis, forward
        )
        high = lax.ppermute(lax.slice_in_dim(block, 0, width, axis=dim), axis, backward)
        block = jnp.concatenate([low, block, high], axis=dim)
    return block


def shifted_views(field, order):
    depth, high, wide, _ = field.shape
    high, wide = high - 2, wide - 2
    lanes = jnp.concatenate([field[:, :, c : c + wide, :] for c in order], axis=-1)
    lanes = jnp.pad(lanes, ((1, 1), (0, 0), (0, 0), (0, 0)))
    if (2 * wide) % 16 == 0:
        return [
            lanes.reshape(depth + 2, (high + 2) * wide, -1),
            lanes[:, 1 : 1 + high].reshape(depth + 2, high * wide, -1),
        ]
    return [lanes[:, b : b + high].reshape(depth + 2, high * wide, -1) for b in range(3)]


def view_at(views, b, pitch):
    if len(views) == 2:
        return (views[1], 0) if b == 1 else (views[0], b * pitch)
    return views[b], 0


def filter_terms(views, pitch, grad_t, out):
    rows = grad_t.shape[1]
    ch = grad_t.shape[0]
    depth = views[0].shape[0] - 2
    plane = rows // depth
    for tap in range(27, out.shape[0]):
        out[tap] = jnp.zeros(out.shape[1:], out.dtype)

    for b in range(3):
        view, start = view_at(views, b, pitch)

        def step(a, _, b=b, view=view, start=start):
            block = view[pl.ds(a, depth), start : start + plane, :].reshape(rows, -1)
            acc = jnp.dot(grad_t[...], block, preferred_element_type=jnp.float32)
            for c in range(3):
                out[9 * a + 3 * b + c] = acc[:, c * ch : (c + 1) * ch].T.astype(out.dtype)
            return 0

        lax.fori_loop(0, 3, step, 0)


def data_plane(views, pitch, weight, acc, x):
    plane, ch = acc.shape
    acc[...] = jnp.zeros_like(acc)

    def step(a, _):
        total = None
        for b in range(3):
            view, start = view_at(views, 2 - b, pitch)
            block = view[x + 2 - a, start : start + plane, :]
            first = pl.multiple_of((9 * a + 3 * b) * ch, 128)
            term = lax.dot_general(
                block,
                weight[:, pl.ds(first, 3 * ch)],
                NT,
                preferred_element_type=jnp.float32,
            )
            total = term if total is None else total + term
        acc[...] += total
        return 0

    lax.fori_loop(0, 3, step, 0)


def enter(sizes):
    barrier = pltpu.get_barrier_semaphore()
    count = 0
    for axis, size in sizes.items():
        me = lax.axis_index(axis)
        for d in range(1, size):
            pl.semaphore_signal(
                barrier, inc=1, device_id={axis: lax.rem(me + d, size)}, device_id_type=MESH
            )
            count += 1
    pl.semaphore_wait(barrier, count)


def fan_out(axis, size, source, target, send, recv):
    me = lax.axis_index(axis)
    copies = []
    for d in range(1, size):
        peer = lax.rem(me + d, size)
        copies.append(
            pltpu.make_async_remote_copy(
                src_ref=source(peer),
                dst_ref=target(d),
                send_sem=send.at[d],
                recv_sem=recv.at[d],
                device_id={axis: peer},
                device_id_type=MESH,
            )
        )
    for copy in copies:
        copy.start()
    return copies


def gather_stages(sizes, shard, whole, sems):
    ndp, nty, ntz = sizes["dp"], sizes["ty"], sizes["tz"]
    dp, ty, tz = lax.axis_index("dp"), lax.axis_index("ty"), lax.axis_index("tz")
    rows, lanes = shard.shape
    part = lanes // (nty * ntz)
    mine = pl.ds(pl.multiple_of((ty * ntz + tz) * part, 128), part)
    group = pl.ds(pl.multiple_of(ty * ntz * part, 128), ntz * part)
    own = pl.ds(pl.multiple_of(dp * rows, 16), rows)

    whole[own, mine] = shard[:, mine]
    copies = fan_out(
        "dp", ndp, lambda peer: shard.at[:, mine], lambda d: whole.at[own, mine], sems.at[0], sems.at[1]
    )
    yield
    for copy in copies:
        copy.wait()
    copies = fan_out(
        "tz", ntz, lambda peer: whole.at[:, mine], lambda d: whole.at[:, mine], sems.at[2], sems.at[3]
    )
    yield
    for copy in copies:
        copy.wait()
    copies = fan_out(
        "ty", nty, lambda peer: whole.at[:, group], lambda d: whole.at[:, group], sems.at[4], sems.at[5]
    )
    yield
    for copy in copies:
        copy.wait()


def reduce_stages(sizes, part, out, bufs, sems):
    ndp, nty, ntz = sizes["dp"], sizes["ty"], sizes["tz"]
    dp, ty, tz = lax.axis_index("dp"), lax.axis_index("ty"), lax.axis_index("tz")
    over_ty, sum_ty, over_tz, sum_tz, over_dp = bufs
    wide, few, rows = sum_ty.shape[0], sum_tz.shape[0], over_dp.shape[2]

    copies = fan_out(
        "ty", nty, lambda peer: part.at[pl.ds(peer * wide, wide)], lambda d: over_ty.at[d - 1],
        sems.at[0], sems.at[1],
    )
    yield
    for copy in copies:
        copy.wait()

    def add_ty(t, _):
        total = part[ty * wide + t].astype(jnp.float32)
        for d in range(nty - 1):
            total += over_ty[d, t].astype(jnp.float32)
        sum_ty[t] = total.astype(sum_ty.dtype)
        return 0

    lax.fori_loop(0, wide, add_ty, 0)
    copies = fan_out(
        "tz", ntz, lambda peer: sum_ty.at[pl.ds(peer * few, few)], lambda d: over_tz.at[d - 1],
        sems.at[2], sems.at[3],
    )
    yield
    for copy in copies:
        copy.wait()

    def add_tz(t, _):
        total = sum_ty[tz * few + t].astype(jnp.float32)
        for d in range(ntz - 1):
            total += over_tz[d, t].astype(jnp.float32)
        sum_tz[t] = total.astype(sum_tz.dtype)
        return 0

    lax.fori_loop(0, few, add_tz, 0)
    copies = fan_out(
        "dp", ndp,
        lambda peer: sum_tz.at[:, pl.ds(pl.multiple_of(peer * rows, 16), rows)],
        lambda d: over_dp.at[d - 1], sems.at[4], sems.at[5],
    )
    yield
    for copy in copies:
        copy.wait()
    first = (ty * ntz + tz) * few

    def add_dp(t, _):
        total = sum_tz[t, pl.ds(pl.multiple_of(dp * rows, 16), rows)].astype(jnp.float32)
        for d in range(ndp - 1):
            total += over_dp[d, t].astype(jnp.float32)
        out[first + t] = total
        return 0

    lax.fori_loop(0, few, add_dp, 0)
    mine = out.at[pl.ds(first, few)]
    copies = fan_out("tz", ntz, lambda peer: mine, lambda d: mine, sems.at[6], sems.at[7])
    yield
    for copy in copies:
        copy.wait()
    group = out.at[pl.ds(ty * wide, wide)]
    copies = fan_out("ty", nty, lambda peer: group, lambda d: group, sems.at[8], sems.at[9])
    yield
    for copy in copies:
        copy.wait()


def advance(stages):
    for stage in stages:
        next(stage, None)


def finish(stages):
    for stage in stages:
        for _ in stage:
            pass


def first_kernel(sizes, pitch, count, *refs):
    views, (grad_t, shard, terms, whole, sems) = refs[:count], refs[count:]
    enter(sizes)
    stages = [gather_stages(sizes, shard, whole, sems)]
    advance(stages)
    filter_terms(views, pitch, grad_t, terms)
    finish(stages)


def terms_kernel(pitch, count, *refs):
    views, (grad_t, terms) = refs[:count], refs[count:]
    filter_terms(views, pitch, grad_t, terms)


def data_kernel(sizes, pitch, count, masked, *refs):
    views, refs = refs[:count], list(refs[count:])
    weight, part = refs[:2]
    del refs[:2]
    if masked:
        pre, shard = refs[:2]
        del refs[:2]
    grad, reduced = refs[:2]
    del refs[:2]
    if masked:
        whole = refs.pop(0)
        gather_sems = refs.pop()
    acc, *bufs, sems = refs
    enter(sizes)
    stages = [reduce_stages(sizes, part, reduced, bufs, sems)]
    if masked:
        stages.append(gather_stages(sizes, shard, whole, gather_sems))
    for x in range(grad.shape[0]):
        advance(stages)
        data_plane(views, pitch, weight, acc, x)
        value = acc[...]
        if masked:
            value = jnp.where(pre[x].astype(jnp.float32) > 0, value, 0.0)
        grad[x] = value.astype(grad.dtype)
    finish(stages)


def local(inputs, pre_first, pre_second, grad_out, w_first, w_second):
    frames, depth, high, wide, ch = grad_out.shape
    sizes = {axis: lax.axis_size(axis) for axis in ("dp", "ty", "tz")}
    ndp, nty, ntz = sizes["dp"], sizes["ty"], sizes["tz"]
    tiles = nty * ntz
    scale = 1.0 / math.sqrt(frames * depth * high * wide * ndp * tiles)
    sides = (("ty", 2), ("tz", 3))
    half = jnp.bfloat16
    rows, plane = depth * high * wide, high * wide
    taps = -(-27 // tiles) * tiles
    few, share = taps // tiles, ch // ndp
    lanes = taps * ch
    shape = jax.ShapeDtypeStruct
    dma = pltpu.SemaphoreType.DMA

    zero_half = jnp.zeros((), half)
    grad_top = jnp.where(pre_second > 0, grad_out, zero_half)
    active = jnp.where(pre_first > 0, pre_first, zero_half)
    padded = extended(jnp.concatenate([active, grad_top, inputs], axis=0), sides, 1)
    forward, backward = (0, 1, 2), (2, 1, 0)
    act_views = shifted_views(padded[0], forward)
    top_views = shifted_views(padded[1], backward)
    in_views = shifted_views(padded[2], forward)
    count = len(act_views)
    shards = [
        jnp.pad(w.reshape(share, -1), ((0, 0), (0, lanes - 27 * ch))) for w in (w_second, w_first)
    ]
    whole_shape = shape((ch, lanes), half)
    terms_shape = shape((taps, ch, ch), half)

    def specs(n):
        return [VMEM] * n

    def run(body, out_shape, scratch, name, operands, collective_id=None):
        params = dict(vmem_limit_bytes=56 * 1024 * 1024)
        if collective_id is not None:
            params.update(collective_id=collective_id, has_side_effects=True)
        return pl.pallas_call(
            body,
            out_shape=out_shape,
            in_specs=specs(len(operands)),
            out_specs=jax.tree.map(lambda _: VMEM, out_shape),
            scratch_shapes=scratch,
            compiler_params=pltpu.CompilerParams(**params),
            name=name,
        )(*operands)

    most = max(sizes.values())
    terms_second, whole_second = run(
        functools.partial(first_kernel, sizes, wide, count),
        (terms_shape, whole_shape),
        [dma((6, most))],
        "terms_second",
        (*act_views, grad_top.reshape(rows, ch).T, shards[0]),
        0,
    )
    reduce_scratch = [
        pltpu.VMEM((plane, ch), jnp.float32),
        pltpu.VMEM((nty - 1, ntz * few, ch, ch), half),
        pltpu.VMEM((ntz * few, ch, ch), half),
        pltpu.VMEM((ntz - 1, few, ch, ch), half),
        pltpu.VMEM((few, ch, ch), half),
        pltpu.VMEM((ndp - 1, few, share, ch), half),
        dma((10, most)),
    ]
    grad_shape = shape((depth, plane, ch), half)
    reduced_shape = shape((taps, share, ch), jnp.float32)
    grad_low, reduced_second, whole_first = run(
        functools.partial(data_kernel, sizes, wide, count, True),
        (grad_shape, reduced_shape, whole_shape),
        [*reduce_scratch, dma((6, most))],
        "grad_low",
        (*top_views, whole_second, terms_second, pre_first.reshape(depth, plane, ch), shards[1]),
        1,
    )
    terms_first = run(
        functools.partial(terms_kernel, wide, count),
        terms_shape,
        [],
        "terms_first",
        (*in_views, grad_low.reshape(rows, ch).T),
    )
    low_views = shifted_views(
        extended(grad_low.reshape(1, depth, high, wide, ch), sides, 1)[0], backward
    )
    grad_input, reduced_first = run(
        functools.partial(data_kernel, sizes, wide, count, False),
        (grad_shape, reduced_shape),
        reduce_scratch,
        "grad_input",
        (*low_views, whole_first, terms_first),
        2,
    )

    def filter_out(reduced):
        return reduced[:27].transpose(1, 0, 2) * scale

    return (
        grad_input.reshape(grad_out.shape),
        filter_out(reduced_first),
        filter_out(reduced_second),
    )


def solution(mesh):
    placed = (
        P("dp", None, "ty", "tz", None),
        P("dp", None, "ty", "tz", None),
        P("dp", None, "ty", "tz", None),
        P("dp", None, "ty", "tz", None),
        P("dp", None, None),
        P("dp", None, None),
    )
    return jax.shard_map(
        local,
        mesh=mesh,
        in_specs=placed,
        out_specs=(P("dp", None, "ty", "tz", None), P("dp", None, None), P("dp", None, None)),
        check_vma=False,
    )
```

```python
import functools
import math

import jax
import jax.numpy as jnp
from jax import lax
from jax.experimental import pallas as pl
from jax.experimental.pallas import tpu as pltpu
from jax.sharding import PartitionSpec as P

MESH = pl.DeviceIdType.MESH
VMEM = pl.BlockSpec(memory_space=pltpu.VMEM)
NT = (((1,), (1,)), ((), ()))


def extended(block, sides, width):
    for axis, dim in sides:
        count = lax.axis_size(axis)
        forward = [(i, i + 1) for i in range(count - 1)]
        backward = [(target, source) for source, target in forward]
        low = lax.ppermute(
            lax.slice_in_dim(block, block.shape[dim] - width, None, axis=dim), axis, forward
        )
        high = lax.ppermute(lax.slice_in_dim(block, 0, width, axis=dim), axis, backward)
        block = jnp.concatenate([low, block, high], axis=dim)
    return block


def shifted_views(field, order):
    depth, high, wide, _ = field.shape
    high, wide = high - 2, wide - 2
    lanes = jnp.concatenate([field[:, :, c : c + wide, :] for c in order], axis=-1)
    lanes = jnp.pad(lanes, ((1, 1), (0, 0), (0, 0), (0, 0)))
    if (2 * wide) % 16 == 0:
        return [
            lanes.reshape(depth + 2, (high + 2) * wide, -1),
            lanes[:, 1 : 1 + high].reshape(depth + 2, high * wide, -1),
        ]
    return [lanes[:, b : b + high].reshape(depth + 2, high * wide, -1) for b in range(3)]


def view_at(views, b, pitch):
    if len(views) == 2:
        return (views[1], 0) if b == 1 else (views[0], b * pitch)
    return views[b], 0


def filter_group(views, pitch, grad_t, out, b):
    ch, rows = grad_t.shape
    depth = views[0].shape[0] - 2
    plane = rows // depth
    view, start = view_at(views, b, pitch)

    def step(a, _):
        block = view[pl.ds(a, depth), start : start + plane, :].reshape(rows, -1)
        acc = jnp.dot(grad_t[...], block, preferred_element_type=jnp.float32)
        for c in range(3):
            out[9 * b + 3 * a + c] = acc[:, c * ch : (c + 1) * ch].T.astype(out.dtype)
        return 0

    lax.fori_loop(0, 3, step, 0)


def data_plane(views, pitch, weight, acc, x):
    plane, ch = acc.shape
    acc[...] = jnp.zeros_like(acc)

    def step(a, _):
        total = None
        for b in range(3):
            view, start = view_at(views, 2 - b, pitch)
            block = view[x + 2 - a, start : start + plane, :]
            first = pl.multiple_of((9 * a + 3 * b) * ch, 128)
            term = lax.dot_general(
                block,
                weight[:, pl.ds(first, 3 * ch)],
                NT,
                preferred_element_type=jnp.float32,
            )
            total = term if total is None else total + term
        acc[...] += total
        return 0

    lax.fori_loop(0, 3, step, 0)


def enter(sizes):
    barrier = pltpu.get_barrier_semaphore()
    count = 0
    for axis, size in sizes.items():
        me = lax.axis_index(axis)
        for d in range(1, size):
            pl.semaphore_signal(
                barrier, inc=1, device_id={axis: lax.rem(me + d, size)}, device_id_type=MESH
            )
            count += 1
    pl.semaphore_wait(barrier, count)


def fan_out(axis, size, source, target, send, recv):
    me = lax.axis_index(axis)
    copies = []
    for d in range(1, size):
        peer = lax.rem(me + d, size)
        copies.append(
            pltpu.make_async_remote_copy(
                src_ref=source(peer),
                dst_ref=target(d),
                send_sem=send.at[d],
                recv_sem=recv.at[d],
                device_id={axis: peer},
                device_id_type=MESH,
            )
        )
    for copy in copies:
        copy.start()
    return copies


def gather_stages(sizes, shard, whole, sems, first, width, over_tiles):
    ndp, nty, ntz = sizes["dp"], sizes["ty"], sizes["tz"]
    dp, ty, tz = lax.axis_index("dp"), lax.axis_index("ty"), lax.axis_index("tz")
    rows = shard.shape[0]
    span = width // nty
    part = span // ntz if over_tiles else span
    start = first + ty * span
    group = pl.ds(pl.multiple_of(start, 128), span)
    mine = pl.ds(pl.multiple_of(start + tz * part, 128), part) if over_tiles else group
    own = pl.ds(pl.multiple_of(dp * rows, 16), rows)

    whole[own, mine] = shard[:, mine]
    copies = fan_out(
        "dp", ndp, lambda peer: shard.at[:, mine], lambda d: whole.at[own, mine], sems.at[0], sems.at[1]
    )
    yield
    for copy in copies:
        copy.wait()
    if over_tiles:
        copies = fan_out(
            "tz", ntz, lambda peer: whole.at[:, mine], lambda d: whole.at[:, mine], sems.at[2], sems.at[3]
        )
        yield
        for copy in copies:
            copy.wait()
    copies = fan_out(
        "ty", nty, lambda peer: whole.at[:, group], lambda d: whole.at[:, group], sems.at[4], sems.at[5]
    )
    yield
    for copy in copies:
        copy.wait()


def added(count, own, others, store):
    def step(t, _):
        total = own(t).astype(jnp.float32)
        for d in range(others.shape[0]):
            total += others[d, t].astype(jnp.float32)
        store(t, total)
        return 0

    lax.fori_loop(0, count, step, 0)


def reduce_stages(sizes, part, out, bufs, sems, first, tz_first):
    ndp, nty, ntz = sizes["dp"], sizes["ty"], sizes["tz"]
    dp, ty, tz = lax.axis_index("dp"), lax.axis_index("ty"), lax.axis_index("tz")
    over_ty, sum_ty, over_tz, second, over_dp = bufs
    wide, rows = sum_ty.shape[0], over_dp.shape[2]
    few = wide // ntz
    begin = first + ty * wide
    slot = begin + tz * few
    own = pl.ds(pl.multiple_of(dp * rows, 16), rows)

    def rows_of(peer):
        return pl.ds(pl.multiple_of(peer * rows, 16), rows)

    def put(target, offset):
        def store(t, total):
            target[offset + t] = total.astype(target.dtype)

        return store

    copies = fan_out(
        "ty", nty, lambda peer: part.at[pl.ds(first + peer * wide, wide)], lambda d: over_ty.at[d - 1],
        sems.at[0], sems.at[1],
    )
    yield
    for copy in copies:
        copy.wait()
    added(wide, lambda t: part[begin + t], over_ty, put(sum_ty, 0))
    if tz_first:
        copies = fan_out(
            "tz", ntz, lambda peer: sum_ty.at[pl.ds(peer * few, few)], lambda d: over_tz.at[d - 1],
            sems.at[2], sems.at[3],
        )
        yield
        for copy in copies:
            copy.wait()
        added(few, lambda t: sum_ty[tz * few + t], over_tz, put(second, 0))
        copies = fan_out(
            "dp", ndp, lambda peer: second.at[:, rows_of(peer)], lambda d: over_dp.at[d - 1],
            sems.at[4], sems.at[5],
        )
        yield
        for copy in copies:
            copy.wait()
        added(few, lambda t: second[t, own], over_dp, put(out, slot))
    else:
        copies = fan_out(
            "dp", ndp, lambda peer: sum_ty.at[:, rows_of(peer)], lambda d: over_dp.at[d - 1],
            sems.at[4], sems.at[5],
        )
        yield
        for copy in copies:
            copy.wait()
        added(wide, lambda t: sum_ty[t, own], over_dp, put(second, 0))
        copies = fan_out(
            "tz", ntz, lambda peer: second.at[pl.ds(peer * few, few)], lambda d: over_tz.at[d - 1],
            sems.at[2], sems.at[3],
        )
        yield
        for copy in copies:
            copy.wait()
        added(few, lambda t: second[tz * few + t], over_tz, put(out, slot))
    mine = out.at[pl.ds(slot, few)]
    copies = fan_out("tz", ntz, lambda peer: mine, lambda d: mine, sems.at[6], sems.at[7])
    yield
    for copy in copies:
        copy.wait()
    group = out.at[pl.ds(begin, wide)]
    copies = fan_out("ty", nty, lambda peer: group, lambda d: group, sems.at[8], sems.at[9])
    yield
    for copy in copies:
        copy.wait()


def advance(stages):
    done = object()
    return [stage for stage in stages if next(stage, done) is not done]


def chains_of(tiles):
    if tiles == 4:
        return [(8, 0, True), (8, 1, False), (8, 2, True), (4, 2, False)]
    return [(16, 1, True), (16, 2, False)]


def layer_kernel(sizes, pitch, count, masked, *refs):
    refs = list(refs)

    def take(n):
        taken = refs[:n]
        del refs[:n]
        return taken

    field_views, data_hbm = take(count), take(count)
    grad_t, shard = take(2)
    pre = take(1)[0] if masked else None
    grad, reduced = take(2)
    data_views = take(count)
    terms, whole, acc, copy_sems, gather_sems, reduce_sems = take(6)

    loads = [
        pltpu.make_async_copy(source, target, copy_sems.at[n])
        for n, (source, target) in enumerate(zip(data_hbm, data_views))
    ]
    for load in loads:
        load.start()
    enter(sizes)
    half = 16 * grad_t.shape[0]
    lanes = shard.shape[1]
    gathers = [
        gather_stages(sizes, shard, whole, gather_sems.at[0], 0, half, True),
        gather_stages(sizes, shard, whole, gather_sems.at[1], half, lanes - half, False),
    ]
    gathers = advance(gathers)
    for tap in range(27, terms.shape[0]):
        terms[tap] = jnp.zeros(terms.shape[1:], terms.dtype)
    reductions = []
    for b in range(3):
        filter_group(field_views, pitch, grad_t, terms, b)
        gathers, reductions = advance(gathers), advance(reductions)
        first = 0
        for n, (slots, after, tz_first) in enumerate(chains_of(sizes["ty"] * sizes["tz"])):
            if after == b:
                bufs = refs[5 * n : 5 * n + 5]
                reductions += advance(
                    [reduce_stages(sizes, terms, reduced, bufs, reduce_sems.at[n], first, tz_first)]
                )
            first += slots
    while gathers:
        gathers = advance(gathers)
    for load in loads:
        load.wait()
    for x in range(grad.shape[0]):
        data_plane(data_views, pitch, whole, acc, x)
        value = acc[...]
        if masked:
            value = jnp.where(pre[x].astype(jnp.float32) > 0, value, 0.0)
        grad[x] = value.astype(grad.dtype)
        reductions = advance(reductions)
    while reductions:
        reductions = advance(reductions)


def local(inputs, pre_first, pre_second, grad_out, w_first, w_second):
    frames, depth, high, wide, ch = grad_out.shape
    sizes = {axis: lax.axis_size(axis) for axis in ("dp", "ty", "tz")}
    ndp, nty, ntz = sizes["dp"], sizes["ty"], sizes["tz"]
    tiles = nty * ntz
    scale = 1.0 / math.sqrt(frames * depth * high * wide * ndp * tiles)
    sides = (("ty", 2), ("tz", 3))
    half = jnp.bfloat16
    rows, plane = depth * high * wide, high * wide
    taps = -(-27 // tiles) * tiles
    share = ch // ndp
    lanes = taps * ch
    shape = jax.ShapeDtypeStruct
    dma = pltpu.SemaphoreType.DMA

    zero_half = jnp.zeros((), half)
    grad_top = jnp.where(pre_second > 0, grad_out, zero_half)
    active = jnp.where(pre_first > 0, pre_first, zero_half)
    padded = extended(jnp.concatenate([active, grad_top, inputs], axis=0), sides, 1)
    forward, backward = (0, 1, 2), (2, 1, 0)
    act_views = shifted_views(padded[0], forward)
    top_views = shifted_views(padded[1], backward)
    in_views = shifted_views(padded[2], forward)
    count = len(act_views)
    shards = [
        jnp.pad(w.reshape(share, -1), ((0, 0), (0, lanes - 27 * ch))) for w in (w_second, w_first)
    ]

    chains = chains_of(tiles)
    most = max(sizes.values())
    scratch = [
        pltpu.VMEM((taps, ch, ch), half),
        pltpu.VMEM((ch, lanes), half),
        pltpu.VMEM((plane, ch), jnp.float32),
        dma((count,)),
        dma((2, 6, most)),
        dma((len(chains), 10, most)),
    ]
    for slots, _, tz_first in chains:
        across = slots // nty
        little = across // ntz
        scratch += [
            pltpu.VMEM((nty - 1, across, ch, ch), half),
            pltpu.VMEM((across, ch, ch), half),
            pltpu.VMEM((ntz - 1, little, ch if tz_first else share, ch), half),
            pltpu.VMEM((little, ch, ch) if tz_first else (across, share, ch), half),
            pltpu.VMEM((ndp - 1, little if tz_first else across, share, ch), half),
        ]
    anywhere = pl.BlockSpec(memory_space=pl.ANY)

    def layer(name, collective_id, field_views, data_views, grad, shard, pre):
        operands = [*field_views, *data_views, grad.reshape(rows, ch).T, shard]
        masked = pre is not None
        if masked:
            operands.append(pre.reshape(depth, plane, ch))
        in_specs = [VMEM] * len(operands)
        in_specs[count : 2 * count] = [anywhere] * count
        return pl.pallas_call(
            functools.partial(layer_kernel, sizes, wide, count, masked),
            out_shape=(shape((depth, plane, ch), half), shape((taps, share, ch), half)),
            in_specs=in_specs,
            out_specs=(VMEM, VMEM),
            scratch_shapes=[pltpu.VMEM(v.shape, half) for v in data_views] + scratch,
            compiler_params=pltpu.CompilerParams(
                vmem_limit_bytes=58 * 1024 * 1024, collective_id=collective_id, has_side_effects=True
            ),
            name=name,
        )(*operands)

    grad_low, reduced_second = layer(
        "second_layer", 0, act_views, top_views, grad_top, shards[0], pre_first
    )
    low_views = shifted_views(
        extended(grad_low.reshape(1, depth, high, wide, ch), sides, 1)[0], backward
    )
    grad_input, reduced_first = layer(
        "first_layer", 1, in_views, low_views, grad_low, shards[1], None
    )

    def filter_out(reduced):
        whole = reduced[:27].reshape(3, 3, 3, share, ch).transpose(3, 1, 0, 2, 4)
        return whole.reshape(share, 27, ch).astype(jnp.float32) * scale

    return (
        grad_input.reshape(grad_out.shape),
        filter_out(reduced_first),
        filter_out(reduced_second),
    )


def solution(mesh):
    placed = (
        P("dp", None, "ty", "tz", None),
        P("dp", None, "ty", "tz", None),
        P("dp", None, "ty", "tz", None),
        P("dp", None, "ty", "tz", None),
        P("dp", None, None),
        P("dp", None, None),
    )
    return jax.shard_map(
        local,
        mesh=mesh,
        in_specs=placed,
        out_specs=(P("dp", None, "ty", "tz", None), P("dp", None, None), P("dp", None, None)),
        check_vma=False,
    )
```

```python
import functools
import math

import jax
import jax.numpy as jnp
from jax import lax
from jax.experimental import pallas as pl
from jax.experimental.pallas import tpu as pltpu
from jax.sharding import PartitionSpec as P

MESH = pl.DeviceIdType.MESH
VMEM = pl.BlockSpec(memory_space=pltpu.VMEM)
NT = (((1,), (1,)), ((), ()))


def extended(block, sides, width):
    for axis, dim in sides:
        count = lax.axis_size(axis)
        forward = [(i, i + 1) for i in range(count - 1)]
        backward = [(target, source) for source, target in forward]
        low = lax.ppermute(
            lax.slice_in_dim(block, block.shape[dim] - width, None, axis=dim), axis, forward
        )
        high = lax.ppermute(lax.slice_in_dim(block, 0, width, axis=dim), axis, backward)
        block = jnp.concatenate([low, block, high], axis=dim)
    return block


def shifted_views(field, order):
    depth, high, wide, _ = field.shape
    high, wide = high - 2, wide - 2
    lanes = jnp.concatenate([field[:, :, c : c + wide, :] for c in order], axis=-1)
    lanes = jnp.pad(lanes, ((1, 1), (0, 0), (0, 0), (0, 0)))
    if (2 * wide) % 16 == 0:
        return [
            lanes.reshape(depth + 2, (high + 2) * wide, -1),
            lanes[:, 1 : 1 + high].reshape(depth + 2, high * wide, -1),
        ]
    return [lanes[:, b : b + high].reshape(depth + 2, high * wide, -1) for b in range(3)]


def view_at(views, b, pitch):
    if len(views) == 2:
        return (views[1], 0) if b == 1 else (views[0], b * pitch)
    return views[b], 0


def filter_group(views, pitch, grad_t, out, b):
    ch, rows = grad_t.shape
    depth = views[0].shape[0] - 2
    plane = rows // depth
    view, start = view_at(views, b, pitch)

    def step(a, _):
        block = view[pl.ds(a, depth), start : start + plane, :].reshape(rows, -1)
        acc = jnp.dot(grad_t[...], block, preferred_element_type=jnp.float32)
        for c in range(3):
            out[9 * b + 3 * a + c] = acc[:, c * ch : (c + 1) * ch].T.astype(out.dtype)
        return 0

    lax.fori_loop(0, 3, step, 0)


def data_plane(views, pitch, weight, acc, x):
    plane, ch = acc.shape
    acc[...] = jnp.zeros_like(acc)

    def step(a, _):
        total = None
        for b in range(3):
            view, start = view_at(views, 2 - b, pitch)
            block = view[x + 2 - a, start : start + plane, :]
            first = pl.multiple_of((9 * a + 3 * b) * ch, 128)
            term = lax.dot_general(
                block,
                weight[:, :, :, pl.ds(first, 3 * ch)].reshape(ch, 3 * ch),
                NT,
                preferred_element_type=jnp.float32,
            )
            total = term if total is None else total + term
        acc[...] += total
        return 0

    lax.fori_loop(0, 3, step, 0)


def enter(sizes):
    barrier = pltpu.get_barrier_semaphore()
    count = 0
    for name in ("lo", "hi", "ty", "tz"):
        me, size, device = place(sizes, name)
        for d in range(1, size):
            pl.semaphore_signal(
                barrier, inc=1, device_id=device(lax.rem(me + d, size)), device_id_type=MESH
            )
            count += 1
    pl.semaphore_wait(barrier, count)


def place(sizes, name):
    if name == "lo":
        dp = lax.axis_index("dp")
        return lax.rem(dp, 2), 2, lambda peer: {"dp": 2 * (dp // 2) + peer}
    if name == "hi":
        dp = lax.axis_index("dp")
        return dp // 2, sizes["dp"] // 2, lambda peer: {"dp": 2 * peer + lax.rem(dp, 2)}
    return lax.axis_index(name), sizes[name], lambda peer: {name: peer}


def fan_out(sizes, name, source, target, send, recv):
    me, size, device = place(sizes, name)
    copies = []
    for d in range(1, size):
        peer = lax.rem(me + d, size)
        copies.append(
            pltpu.make_async_remote_copy(
                src_ref=source(peer),
                dst_ref=target(d),
                send_sem=send.at[d],
                recv_sem=recv.at[d],
                device_id=device(peer),
                device_id_type=MESH,
            )
        )
    for copy in copies:
        copy.start()
    return copies


def gather_stages(sizes, shard, whole, sems, first, width, over_tiles):
    nty, ntz = sizes["ty"], sizes["tz"]
    ty, tz = lax.axis_index("ty"), lax.axis_index("tz")
    hi, lo = place(sizes, "hi")[0], place(sizes, "lo")[0]
    span = width // nty
    part = span // ntz if over_tiles else span
    start = first + ty * span
    group = pl.ds(pl.multiple_of(start, 128), span)
    mine = pl.ds(pl.multiple_of(start + tz * part, 128), part) if over_tiles else group

    whole[hi, lo, :, mine] = shard[:, mine]
    steps = [
        ("hi", shard.at[:, mine], whole.at[hi, lo, :, mine]),
        ("lo", whole.at[:, lo, :, mine], whole.at[:, lo, :, mine]),
    ]
    if over_tiles:
        steps.append(("tz", whole.at[:, :, :, mine], whole.at[:, :, :, mine]))
    steps.append(("ty", whole.at[:, :, :, group], whole.at[:, :, :, group]))
    for n, (name, source, target) in enumerate(steps):
        copies = fan_out(
            sizes, name, lambda peer: source, lambda d: target, sems.at[2 * n], sems.at[2 * n + 1]
        )
        yield
        for copy in copies:
            copy.wait()


def added(count, own, others, store):
    def step(t, _):
        total = own(t).astype(jnp.float32)
        for d in range(others.shape[0]):
            total += others[d, t].astype(jnp.float32).reshape(total.shape)
        store(t, total)
        return 0

    lax.fori_loop(0, count, step, 0)


def reduce_stages(sizes, part, out, bufs, sems, first, tz_first):
    nty, ntz = sizes["ty"], sizes["tz"]
    ty, tz = lax.axis_index("ty"), lax.axis_index("tz")
    hi, lo = place(sizes, "hi")[0], place(sizes, "lo")[0]
    over_ty, sum_ty, over_tz, sum_tz, over_lo, sum_lo, over_hi = bufs
    wide = sum_ty.shape[0]
    few = wide // ntz
    begin = first + ty * wide
    slot = begin + tz * few

    def put(target, offset):
        def store(t, total):
            target[offset + t] = total.reshape(target.shape[1:]).astype(target.dtype)

        return store

    def send(n, name, source, target):
        return fan_out(sizes, name, source, target, sems.at[2 * n], sems.at[2 * n + 1])

    copies = send(
        0, "ty", lambda peer: part.at[pl.ds(first + peer * wide, wide)], lambda d: over_ty.at[d - 1]
    )
    yield
    for copy in copies:
        copy.wait()
    added(wide, lambda t: part[begin + t], over_ty, put(sum_ty, 0))
    held, count = sum_ty, wide
    if tz_first:
        copies = send(
            1, "tz", lambda peer: sum_ty.at[pl.ds(peer * few, few)], lambda d: over_tz.at[d - 1]
        )
        yield
        for copy in copies:
            copy.wait()
        added(few, lambda t: sum_ty[tz * few + t], over_tz, put(sum_tz, 0))
        held, count = sum_tz, few
    copies = send(2, "lo", lambda peer: held.at[:, :, peer], lambda d: over_lo.at[d - 1])
    yield
    for copy in copies:
        copy.wait()
    added(count, lambda t: held[t, :, lo], over_lo, put(sum_lo, 0))
    copies = send(3, "hi", lambda peer: sum_lo.at[:, peer], lambda d: over_hi.at[d - 1])
    yield
    for copy in copies:
        copy.wait()
    if tz_first:
        added(few, lambda t: sum_lo[t, hi], over_hi, put(out, slot))
    else:
        added(wide, lambda t: sum_lo[t, hi], over_hi, put(sum_tz, 0))
        copies = send(
            1, "tz", lambda peer: sum_tz.at[pl.ds(peer * few, few)], lambda d: over_tz.at[d - 1]
        )
        yield
        for copy in copies:
            copy.wait()
        added(few, lambda t: sum_tz[tz * few + t], over_tz, put(out, slot))
    mine = out.at[pl.ds(slot, few)]
    copies = send(4, "tz", lambda peer: mine, lambda d: mine)
    yield
    for copy in copies:
        copy.wait()
    group = out.at[pl.ds(begin, wide)]
    copies = send(5, "ty", lambda peer: group, lambda d: group)
    yield
    for copy in copies:
        copy.wait()


def advance(stages):
    done = object()
    return [stage for stage in stages if next(stage, done) is not done]


def chains_of(tiles):
    if tiles == 4:
        return [(8, 0, True), (8, 1, False), (8, 2, True), (4, 2, False)]
    return [(16, 1, True), (16, 2, False)]


def layer_kernel(sizes, pitch, count, masked, *refs):
    refs = list(refs)

    def take(n):
        taken = refs[:n]
        del refs[:n]
        return taken

    field_views, data_hbm = take(count), take(count)
    grad_t, shard = take(2)
    pre = take(1)[0] if masked else None
    grad, reduced = take(2)
    data_views = take(count)
    terms, whole, acc, copy_sems, gather_sems, reduce_sems = take(6)

    loads = [
        pltpu.make_async_copy(source, target, copy_sems.at[n])
        for n, (source, target) in enumerate(zip(data_hbm, data_views))
    ]
    for load in loads:
        load.start()
    enter(sizes)
    half = 16 * grad_t.shape[0]
    lanes = shard.shape[1]
    gathers = [
        gather_stages(sizes, shard, whole, gather_sems.at[0], 0, half, True),
        gather_stages(sizes, shard, whole, gather_sems.at[1], half, lanes - half, False),
    ]
    gathers = advance(gathers)
    for tap in range(27, terms.shape[0]):
        terms[tap] = jnp.zeros(terms.shape[1:], terms.dtype)
    reductions = []
    for b in range(3):
        filter_group(field_views, pitch, grad_t, terms, b)
        gathers, reductions = advance(gathers), advance(reductions)
        first = 0
        for n, (slots, after, tz_first) in enumerate(chains_of(sizes["ty"] * sizes["tz"])):
            if after == b:
                bufs = refs[7 * n : 7 * n + 7]
                reductions += advance(
                    [reduce_stages(sizes, terms, reduced, bufs, reduce_sems.at[n], first, tz_first)]
                )
            first += slots
    while gathers:
        gathers = advance(gathers)
    for load in loads:
        load.wait()
    for x in range(grad.shape[0]):
        data_plane(data_views, pitch, whole, acc, x)
        value = acc[...]
        if masked:
            value = jnp.where(pre[x].astype(jnp.float32) > 0, value, 0.0)
        grad[x] = value.astype(grad.dtype)
        reductions = advance(reductions)
    while reductions:
        reductions = advance(reductions)


def local(inputs, pre_first, pre_second, grad_out, w_first, w_second):
    frames, depth, high, wide, ch = grad_out.shape
    sizes = {axis: lax.axis_size(axis) for axis in ("dp", "ty", "tz")}
    ndp, nty, ntz = sizes["dp"], sizes["ty"], sizes["tz"]
    tiles = nty * ntz
    scale = 1.0 / math.sqrt(frames * depth * high * wide * ndp * tiles)
    sides = (("ty", 2), ("tz", 3))
    half = jnp.bfloat16
    rows, plane = depth * high * wide, high * wide
    taps = -(-27 // tiles) * tiles
    share = ch // ndp
    lanes = taps * ch
    shape = jax.ShapeDtypeStruct
    dma = pltpu.SemaphoreType.DMA

    zero_half = jnp.zeros((), half)
    grad_top = jnp.where(pre_second > 0, grad_out, zero_half)
    active = jnp.where(pre_first > 0, pre_first, zero_half)
    padded = extended(jnp.concatenate([active, grad_top, inputs], axis=0), sides, 1)
    forward, backward = (0, 1, 2), (2, 1, 0)
    act_views = shifted_views(padded[0], forward)
    top_views = shifted_views(padded[1], backward)
    in_views = shifted_views(padded[2], forward)
    count = len(act_views)
    shards = [
        jnp.pad(w.reshape(share, -1), ((0, 0), (0, lanes - 27 * ch))) for w in (w_second, w_first)
    ]

    chains = chains_of(tiles)
    most = max(sizes.values())
    highs = ndp // 2
    scratch = [
        pltpu.VMEM((taps, ch, ch), half),
        pltpu.VMEM((highs, 2, share, lanes), half),
        pltpu.VMEM((plane, ch), jnp.float32),
        dma((count,)),
        dma((2, 8, most)),
        dma((len(chains), 12, most)),
    ]
    for slots, _, tz_first in chains:
        across = slots // nty
        little = across // ntz
        scratch += [
            pltpu.VMEM((nty - 1, across, ch, ch), half),
            pltpu.VMEM((across, highs, 2, share, ch), half),
            pltpu.VMEM((ntz - 1, little, *((highs, 2) if tz_first else ()), share, ch), half),
            pltpu.VMEM((little, highs, 2, share, ch) if tz_first else (across, share, ch), half),
            pltpu.VMEM((1, little if tz_first else across, highs, share, ch), half),
            pltpu.VMEM((little if tz_first else across, highs, share, ch), half),
            pltpu.VMEM((highs - 1, little if tz_first else across, share, ch), half),
        ]
    anywhere = pl.BlockSpec(memory_space=pl.ANY)

    def layer(name, collective_id, field_views, data_views, grad, shard, pre):
        operands = [*field_views, *data_views, grad.reshape(rows, ch).T, shard]
        masked = pre is not None
        if masked:
            operands.append(pre.reshape(depth, plane, ch))
        in_specs = [VMEM] * len(operands)
        in_specs[count : 2 * count] = [anywhere] * count
        return pl.pallas_call(
            functools.partial(layer_kernel, sizes, wide, count, masked),
            out_shape=(shape((depth, plane, ch), half), shape((taps, share, ch), half)),
            in_specs=in_specs,
            out_specs=(VMEM, VMEM),
            scratch_shapes=[pltpu.VMEM(v.shape, half) for v in data_views] + scratch,
            compiler_params=pltpu.CompilerParams(
                vmem_limit_bytes=58 * 1024 * 1024, collective_id=collective_id, has_side_effects=True
            ),
            name=name,
        )(*operands)

    grad_low, reduced_second = layer(
        "second_layer", 0, act_views, top_views, grad_top, shards[0], pre_first
    )
    low_views = shifted_views(
        extended(grad_low.reshape(1, depth, high, wide, ch), sides, 1)[0], backward
    )
    grad_input, reduced_first = layer(
        "first_layer", 1, in_views, low_views, grad_low, shards[1], None
    )

    def filter_out(reduced):
        whole = reduced[:27].reshape(3, 3, 3, share, ch).transpose(3, 1, 0, 2, 4)
        return whole.reshape(share, 27, ch).astype(jnp.float32) * scale

    return (
        grad_input.reshape(grad_out.shape),
        filter_out(reduced_first),
        filter_out(reduced_second),
    )


def solution(mesh):
    placed = (
        P("dp", None, "ty", "tz", None),
        P("dp", None, "ty", "tz", None),
        P("dp", None, "ty", "tz", None),
        P("dp", None, "ty", "tz", None),
        P("dp", None, None),
        P("dp", None, None),
    )
    return jax.shard_map(
        local,
        mesh=mesh,
        in_specs=placed,
        out_specs=(P("dp", None, "ty", "tz", None), P("dp", None, None), P("dp", None, None)),
        check_vma=False,
    )
```
